32 devices in a mesh: gx: 4 (over y, x), gy: 8 (over z, core).
Axes of the slice: x: 2, y: 2, z: 4, core: 2. Of those that a mesh axis runs over, the one named last changes fastest.
Arguments:
- noisy_state: bfloat16 [4, 2048, 512], P(None, 'gy', 'gx'), may hold values from -6 to 6
- fresh_noise: bfloat16 [4, 2048, 512], P(None, 'gy', 'gx'), may hold values from -6 to 6
- conditioning: bfloat16 [12, 2048, 512], P(None, 'gy', 'gx'), may hold values from -6 to 6
- first_kernel: bfloat16 [3, 3, 128, 16], replicated, may hold values from -0.5 to 0.5
- first_bias: float32 [128], replicated, may hold values from -4 to 4
- film_weight: bfloat16 [256, 12], replicated, may hold values from -1.75 to 1.75
- film_bias: float32 [256], replicated, may hold values from -3 to 3
- second_kernel: bfloat16 [3, 3, 128, 128], replicated, may hold values from -0.1875 to 0.1875
- second_bias: float32 [128], replicated, may hold values from -4 to 4
- skip_kernel: bfloat16 [128, 16], replicated, may hold values from -1.5 to 1.5
- out_kernel: bfloat16 [4, 128], replicated, may hold values from -0.5 to 0.5
- strip_table: bfloat16 [160, 1024], P('gx'), may hold values from -6 to 6
- segment_rows: int32 [160], replicated, may hold values from 0 to 159, each once
- step_index: int32 [1], replicated, may hold values from 10 to 13
Outputs:
- next_state: bfloat16 [4, 2048, 512], P(None, 'gy', 'gx')
The draws below stay inside these ranges and needn't reach their ends.
Inputs may be any that keep to these rules, and one draw needn't show every extreme that they name: `segment_rows`: each strip row feeds exactly one of the 160 boundary segments.
All inputs are finite; a program needn't handle non-finite values.
Results may differ from the reference program's by a relative error of at most 0.0049.
Values may be sent and summed in bfloat16 or wider, within the bound.
A program may use at most 192 MiB of HBM per device.

```python
import jax
import jax.numpy as jnp
from jax import lax

CT = 4
C = 128
COND = 12
HT = 256
SEG = 32
BAND = 8
NSTEPS = 18
NX = 512
NY = 2048
NSEG = 160


def shard_levels(key, shape, cuts, smallest, high):
    def one(axis_at, blocks):
        draws = jax.random.uniform(jax.random.fold_in(jax.random.fold_in(key, 6), axis_at), (blocks,), jnp.float32, smallest / len(cuts), high / len(cuts))
        return jnp.repeat(jnp.exp(draws), shape[axis_at] // blocks).reshape((-1,) + (1,) * (len(shape) - axis_at - 1))

    gain = one(*cuts[0])
    for cut in cuts[1:]:
        gain = gain * one(*cut)
    return gain


def bell_draw(rng, dims, scale, bound, pieces=(), kind=jnp.bfloat16):
    drawn = scale * jax.random.normal(rng, dims, jnp.float32)
    if pieces:
        drawn = drawn * shard_levels(rng, dims, pieces, -0.22, 0.18)
    return jnp.clip(drawn, -bound, bound).astype(kind)


def setup_inputs(seed: int = 0) -> dict:
    key_list = jax.random.split(jax.random.key(seed), 15)
    return {
        "noisy_state": bell_draw(key_list[0], (CT, NY, NX), 1.0, 6.0, ((1, 8), (2, 4))),
        "fresh_noise": bell_draw(key_list[1], (CT, NY, NX), 1.0, 6.0, ((1, 8), (2, 4))),
        "conditioning": bell_draw(key_list[2], (COND, NY, NX), 1.0, 6.0, ((1, 8), (2, 4))),
        "first_kernel": bell_draw(key_list[3], (3, 3, C, CT + COND), (9 * (CT + COND)) ** -0.5, 0.5),
        "first_bias": bell_draw(key_list[4], (C,), 1.0, 4.0, (), jnp.float32),
        "film_weight": bell_draw(key_list[5], (2 * C, COND), COND ** -0.5, 1.75),
        "film_bias": bell_draw(key_list[6], (2 * C,), 0.5, 3.0, (), jnp.float32),
        "second_kernel": bell_draw(key_list[7], (3, 3, C, C), (9 * C) ** -0.5, 0.1875),
        "second_bias": bell_draw(key_list[8], (C,), 1.0, 4.0, (), jnp.float32),
        "skip_kernel": bell_draw(key_list[9], (C, CT + COND), (CT + COND) ** -0.5, 1.5),
        "out_kernel": bell_draw(key_list[10], (CT, C), C ** -0.5, 0.5),
        "strip_table": bell_draw(key_list[11], (NSEG, CT * BAND * SEG), 1.0, 6.0, ((0, 4),)),
        "segment_rows": jax.random.permutation(key_list[12], NSEG).astype(jnp.int32),
        "step_index": jax.random.randint(key_list[13], (1,), 10, 14).astype(jnp.int32),
    }


SIGMA_MAX = 800.0
SIGMA_MIN = 0.002
RHO_POWER = 7.0
CHURN_GAIN = 0.25
NOISE_GAIN = 1.007
SIGMA_DATA = 0.5
RELAX_GAIN = 3.0
ROOT_HALF = 0.7071067811865476

def noise_levels(step_index, total_steps):
    upper_root = SIGMA_MAX ** (1.0 / RHO_POWER)
    lower_root = SIGMA_MIN ** (1.0 / RHO_POWER)
    position = step_index[0].astype(jnp.float32)
    sigma_now = (upper_root + position / (total_steps - 1) * (lower_root - upper_root)) ** RHO_POWER
    sigma_next = (upper_root + (position + 1.0) / (total_steps - 1) * (lower_root - upper_root)) ** RHO_POWER
    return (sigma_now, sigma_next)

def sampler_terms(step_index):
    sigma_now, sigma_next = noise_levels(step_index, NSTEPS)
    sigma_hat = (1.0 + CHURN_GAIN) * sigma_now
    spread = NOISE_GAIN * jnp.sqrt(sigma_hat * sigma_hat - sigma_now * sigma_now)
    energy = sigma_hat * sigma_hat + SIGMA_DATA * SIGMA_DATA
    scale_in = 1.0 / jnp.sqrt(energy)
    scale_skip = SIGMA_DATA * SIGMA_DATA / energy
    scale_out = sigma_hat * SIGMA_DATA / jnp.sqrt(energy)
    stride = (sigma_next - sigma_hat) / sigma_hat
    return (spread, scale_in, scale_skip, scale_out, stride)

def relax_weight(distance, band):
    return jnp.where((distance >= 0) & (distance < band), RELAX_GAIN * (band - distance) / band, 0.0)

def conv_taps(padded, kernel, out_rows, out_cols):
    summed = jnp.zeros((kernel.shape[2], out_rows, out_cols), jnp.float32)
    for offset_row in range(3):
        for offset_col in range(3):
            window = padded[:, offset_row:offset_row + out_rows, offset_col:offset_col + out_cols].astype(jnp.float32)
            summed = summed + jnp.einsum('oc,chw->ohw', kernel[offset_row, offset_col].astype(jnp.float32), window)
    return summed

def side_values(table, first_seg, seg_total, length):
    chosen = table[first_seg:first_seg + seg_total]
    return chosen.transpose(1, 2, 0, 3).reshape(table.shape[1], table.shape[2], length)

def reference(noisy_state, fresh_noise, conditioning, first_kernel, first_bias, film_weight, film_bias, second_kernel, second_bias, skip_kernel, out_kernel, strip_table, segment_rows, step_index):
    spread, scale_in, scale_skip, scale_out, stride = sampler_terms(step_index)
    segs_wide = NX // SEG
    segs_tall = NY // SEG
    table = jnp.take(strip_table, segment_rows, axis=0).reshape(NSEG, CT, BAND, SEG)
    south_side = side_values(table, 0, segs_wide, NX)
    north_side = side_values(table, segs_wide, segs_wide, NX)
    west_side = side_values(table, 2 * segs_wide, segs_tall, NY)
    east_side = side_values(table, 2 * segs_wide + segs_tall, segs_tall, NY)
    band_weight = relax_weight(jnp.arange(BAND, dtype=jnp.float32), BAND)
    global_cols = jnp.arange(NX, dtype=jnp.float32)
    col_weight = relax_weight(global_cols, BAND) + relax_weight(NX - 1.0 - global_cols, BAND)

    def one_block(block_index):
        first_row = block_index * HT
        row_ids = first_row - 2 + jnp.arange(HT + 4, dtype=jnp.int32)
        inside = (row_ids >= 0) & (row_ids < NY)
        clipped = jnp.clip(row_ids, 0, NY - 1)
        state_rows = jnp.take(noisy_state, clipped, axis=1).astype(jnp.float32)
        noise_rows = jnp.take(fresh_noise, clipped, axis=1).astype(jnp.float32)
        cond_rows = jnp.take(conditioning, clipped, axis=1)
        state_hat = state_rows + spread * noise_rows
        net_in = jnp.concatenate([scale_in * state_hat, cond_rows.astype(jnp.float32)], axis=0)
        net_in = jnp.where(inside[None, :, None], net_in, 0.0).astype(jnp.bfloat16)
        padded = jnp.pad(net_in, ((0, 0), (0, 0), (1, 1)))
        first_act = conv_taps(padded, first_kernel, HT + 2, NX) + first_bias[:, None, None]
        modulation = jnp.einsum('mc,chw->mhw', film_weight.astype(jnp.float32), cond_rows[:, 1:-1, :].astype(jnp.float32)) + film_bias[:, None, None]
        shaped = first_act * (1.0 + modulation[:C]) + modulation[C:]
        hidden = jnp.where(inside[1:-1][None, :, None], jax.nn.silu(shaped), 0.0).astype(jnp.bfloat16)
        second_act = conv_taps(jnp.pad(hidden, ((0, 0), (0, 0), (1, 1))), second_kernel, HT, NX) + second_bias[:, None, None]
        skip_path = jnp.einsum('oc,chw->ohw', skip_kernel.astype(jnp.float32), net_in[:, 2:-2, :].astype(jnp.float32))
        branch = ((skip_path + second_act) * ROOT_HALF).astype(jnp.bfloat16)
        projected = jnp.einsum('oc,chw->ohw', out_kernel.astype(jnp.float32), branch.astype(jnp.float32))
        centre = state_hat[:, 2:-2, :]
        denoised = scale_skip * centre + scale_out * projected
        global_rows = first_row + jnp.arange(HT, dtype=jnp.int32)
        from_south = global_rows.astype(jnp.float32)
        south_weight = relax_weight(from_south, BAND)
        north_weight = relax_weight(NY - 1.0 - from_south, BAND)
        south_rows = jnp.take(south_side, jnp.clip(global_rows, 0, BAND - 1), axis=1).astype(jnp.float32)
        north_rows = jnp.take(north_side, jnp.clip(NY - 1 - global_rows, 0, BAND - 1), axis=1).astype(jnp.float32)
        west_rows = jnp.take(west_side, global_rows, axis=2).astype(jnp.float32).transpose(0, 2, 1)
        east_rows = jnp.take(east_side, global_rows, axis=2).astype(jnp.float32).transpose(0, 2, 1)[:, :, ::-1]
        numerator = denoised + south_weight[None, :, None] * south_rows + north_weight[None, :, None] * north_rows
        numerator = numerator.at[:, :, :BAND].add(band_weight[None, None, :] * west_rows)
        numerator = numerator.at[:, :, NX - BAND:].add(band_weight[::-1][None, None, :] * east_rows)
        denominator = 1.0 + south_weight[:, None] + north_weight[:, None] + col_weight[None, :]
        relaxed = numerator / denominator[None]
        return (centre + stride * (centre - relaxed)).astype(jnp.bfloat16)
    blocks = lax.map(one_block, jnp.arange(NY // HT, dtype=jnp.int32))
    return blocks.transpose(1, 0, 2, 3).reshape(CT, NY, NX)
```

```python
import functools

import jax
import jax.numpy as jnp
from jax import lax
from jax.experimental import pallas as pl
from jax.experimental.pallas import tpu as pltpu
from jax.sharding import PartitionSpec as P

SEG = 32
BAND = 8
NSTEPS = 18


SIGMA_MAX = 800.0
SIGMA_MIN = 0.002
RHO_POWER = 7.0
CHURN_GAIN = 0.25
NOISE_GAIN = 1.007
SIGMA_DATA = 0.5
RELAX_GAIN = 3.0
ROOT_HALF = 0.7071067811865476


def shifted(block, axis, step):
    count = lax.axis_size(axis)
    if step > 0:
        pairs = [(i, i + 1) for i in range(count - 1)]
    else:
        pairs = [(i + 1, i) for i in range(count - 1)]
    return lax.ppermute(block, axis, pairs)


def with_halo(net_in):
    cols = net_in.shape[2]
    left = shifted(net_in[:, :, cols - 2 :].transpose(2, 0, 1), "gx", 1)
    right = shifted(net_in[:, :, :2].transpose(2, 0, 1), "gx", -1)
    wide = jnp.concatenate(
        [left.transpose(2, 1, 0), net_in.transpose(1, 0, 2), right.transpose(2, 1, 0)], axis=2
    )
    rows = wide.shape[0]
    above = shifted(wide[rows - 2 :], "gy", 1)
    below = shifted(wide[:2], "gy", -1)
    return jnp.concatenate([above, wide, below], axis=0)


def three_parts(values):
    high = lax.reduce_precision(values, 8, 7)
    rest = values - high
    mid = lax.reduce_precision(rest, 8, 7)
    return jnp.stack([high, mid, rest - mid]).astype(jnp.bfloat16)


def bias_rows(values):
    return jnp.pad(three_parts(values), ((0, 13), (0, 0)))


def first_weights(first_kernel, first_bias, film_weight, film_bias):
    width, inner = first_kernel.shape[2], first_kernel.shape[3]
    taps = first_kernel.transpose(1, 0, 3, 2)
    conv = jnp.concatenate(
        [jnp.pad(taps, ((0, 0), (s, 1 - s), (0, 0), (0, 0))) for s in (0, 1)], axis=3
    ).reshape(12 * inner, 2 * width)
    lead = inner - film_weight.shape[1]
    film = jnp.pad(film_weight.T, ((lead, 0), (0, 0)))
    parts = [conv]
    for k in (0, 1):
        piece = film[:, k * width : (k + 1) * width]
        both = jnp.concatenate(
            [jnp.pad(piece, ((inner * (5 + s), inner * (6 - s)), (0, 0))) for s in (0, 1)], axis=1
        )
        parts.append(both)
    parts = [parts[0]] + parts[1:]
    biases = [first_bias, 1.0 + film_bias[:width], film_bias[width:]]
    row = jnp.concatenate([jnp.tile(v, 2) for v in biases])
    return jnp.concatenate([jnp.concatenate(parts, axis=1), bias_rows(row)], axis=0)


def second_weights(second_kernel):
    width, inner = second_kernel.shape[2], second_kernel.shape[3]
    taps = second_kernel.transpose(0, 1, 3, 2).reshape(3, 3 * inner, width)
    return jnp.concatenate(
        [jnp.pad(taps, ((s, 1 - s), (0, 0), (0, 0))) for s in (0, 1)], axis=2
    ).reshape(12 * inner, 2 * width)


def skip_weights(skip_kernel, second_bias):
    width, inner = skip_kernel.shape
    flat = skip_kernel.T
    both = jnp.concatenate(
        [jnp.pad(flat, ((inner * s, inner * (1 - s)), (0, 0))) for s in (0, 1)], axis=1
    )
    return jnp.concatenate([both, bias_rows(jnp.tile(second_bias, 2))], axis=0)


def out_weights(out_kernel):
    width = out_kernel.shape[1]
    return jnp.concatenate(
        [jnp.pad(out_kernel, ((0, 0), (width * s, width * (1 - s)))) for s in (0, 1)], axis=0
    )


def block_kernel(pairs, group, cols, width, net_ref, first_ref, second_ref, skip_ref, out_ref,
                 proj_ref, held):
    tile_col, tile_row = lax.axis_index("gx"), lax.axis_index("gy")
    last_col, last_row = lax.axis_size("gx") - 1, lax.axis_size("gy") - 1
    wide = net_ref.shape[2]
    place = lax.broadcasted_iota(jnp.int32, (wide, width), 0)
    low = jnp.where(tile_col == 0, 1, 0)
    high = jnp.where(tile_col == last_col, cols, cols + 1)
    col_mask = ((place >= low) & (place <= high)).astype(jnp.float32)
    ones = jnp.ones((16, wide), jnp.bfloat16)

    def hidden_pair(i, slot):
        start = pl.multiple_of(i * 32, 32)
        patch = jnp.concatenate([net_ref[b, pl.ds(start, 64), :] for b in range(3)] + [ones], axis=0)
        act = lax.dot_general(
            patch, first_ref[...], (((0,), (0,)), ((), ())), preferred_element_type=jnp.float32
        )
        for s in range(2):
            lo = s * width
            shaped = (
                act[:, lo : lo + width] * act[:, 2 * width + lo : 3 * width + lo]
                + act[:, 4 * width + lo : 5 * width + lo]
            )
            half = 0.5 * shaped
            value = half * jnp.tanh(half) + half
            if s == 0:
                inside = jnp.where((i == 0) & (tile_row == 0), 0.0, 1.0)
            else:
                inside = jnp.where((i == pairs) & (tile_row == last_row), 0.0, 1.0)
            value = value * (col_mask * inside)
            for b in range(3):
                moved = value if b == 0 else pltpu.roll(value, wide - b, 0)
                at = (s * 3 + b) * width
                held[slot, :, at : at + width] = moved[:cols].astype(jnp.bfloat16)

    def out_pair(i, slot):
        start = pl.multiple_of(i * 32 + 32, 32)
        centre = jnp.concatenate([net_ref[2, pl.ds(start, 32), :cols], ones[:, :cols]], axis=0)
        depth = 6 * width
        total = jnp.dot(held[slot], second_ref[:depth], preferred_element_type=jnp.float32)
        total += jnp.dot(held[slot + 1], second_ref[depth:], preferred_element_type=jnp.float32)
        total += lax.dot_general(
            centre, skip_ref[...], (((0,), (0,)), ((), ())), preferred_element_type=jnp.float32
        )
        branch = (total * ROOT_HALF).astype(jnp.bfloat16)
        proj_ref[i] = lax.dot_general(
            out_ref[...], branch, (((1,), (1,)), ((), ())), preferred_element_type=jnp.float32
        )

    hidden_pair(jnp.int32(0), 0)

    @pl.loop(0, pairs // group)
    def _(step):
        for k in range(group):
            hidden_pair(step * group + k + 1, k + 1)
            out_pair(step * group + k, k)
        held[0] = held[group]


def residual_block(ext, first_w, second_w, skip_w, out_w, cols):
    rows_ext, inner, cols_ext = ext.shape
    pairs = (rows_ext - 4) // 2
    width = second_w.shape[1] // 2
    wide = cols + 16
    group = 4
    flat = ext.reshape(rows_ext * inner, cols_ext)
    flat = jnp.pad(flat, ((0, 0), (0, wide + 2 - cols_ext)))
    net3 = jnp.stack([flat[:, b : b + wide] for b in range(3)])
    return pl.pallas_call(
        functools.partial(block_kernel, pairs, group, cols, width),
        out_shape=jax.ShapeDtypeStruct((pairs, out_w.shape[0], cols), jnp.float32),
        in_specs=[pl.BlockSpec(memory_space=pltpu.VMEM)] * 5,
        out_specs=pl.BlockSpec(memory_space=pltpu.VMEM),
        scratch_shapes=[pltpu.VMEM((group + 1, cols, 6 * width), jnp.bfloat16)],
        compiler_params=pltpu.CompilerParams(vmem_limit_bytes=48 * 1024 * 1024),
    )(net3, first_w, second_w, skip_w, out_w)


def noise_levels(step_index, total_steps):
    upper_root = SIGMA_MAX ** (1.0 / RHO_POWER)
    lower_root = SIGMA_MIN ** (1.0 / RHO_POWER)
    position = step_index[0].astype(jnp.float32)
    sigma_now = (upper_root + position / (total_steps - 1) * (lower_root - upper_root)) ** RHO_POWER
    sigma_next = (
        upper_root + (position + 1.0) / (total_steps - 1) * (lower_root - upper_root)
    ) ** RHO_POWER
    return (sigma_now, sigma_next)


def sampler_terms(step_index):
    sigma_now, sigma_next = noise_levels(step_index, NSTEPS)
    sigma_hat = (1.0 + CHURN_GAIN) * sigma_now
    spread = NOISE_GAIN * jnp.sqrt(sigma_hat * sigma_hat - sigma_now * sigma_now)
    energy = sigma_hat * sigma_hat + SIGMA_DATA * SIGMA_DATA
    scale_in = 1.0 / jnp.sqrt(energy)
    scale_skip = SIGMA_DATA * SIGMA_DATA / energy
    scale_out = sigma_hat * SIGMA_DATA / jnp.sqrt(energy)
    stride = (sigma_next - sigma_hat) / sigma_hat
    return (spread, scale_in, scale_skip, scale_out, stride)


def relax_weight(distance, band):
    return jnp.where(
        (distance >= 0) & (distance < band), RELAX_GAIN * (band - distance) / band, 0.0
    )


def side_values(table, first_seg, seg_total, length):
    chosen = table[first_seg : first_seg + seg_total]
    return chosen.transpose(1, 2, 0, 3).reshape(table.shape[1], table.shape[2], length)


def boundary_ids(col_ids, row_ids, col_count, row_count, segs_wide, segs_tall, segment_rows):
    seg_total = segment_rows.shape[0]
    along_wide = jnp.arange(segs_wide, dtype=jnp.int32)[None, :]
    along_tall = jnp.arange(segs_tall, dtype=jnp.int32)[None, :]
    wide_all = col_count * segs_wide
    tall_all = row_count * segs_tall
    south_segs = col_ids[:, None] * segs_wide + along_wide
    north_segs = wide_all + col_ids[:, None] * segs_wide + along_wide
    west_segs = 2 * wide_all + row_ids[:, None] * segs_tall + along_tall
    east_segs = 2 * wide_all + tall_all + row_ids[:, None] * segs_tall + along_tall
    seg_ids = jnp.concatenate([south_segs, north_segs, west_segs, east_segs], axis=1)
    valid = jnp.concatenate(
        [
            jnp.broadcast_to((row_ids == 0)[:, None], south_segs.shape),
            jnp.broadcast_to((row_ids == row_count - 1)[:, None], north_segs.shape),
            jnp.broadcast_to((col_ids == 0)[:, None], west_segs.shape),
            jnp.broadcast_to((col_ids == col_count - 1)[:, None], east_segs.shape),
        ],
        axis=1,
    )
    matches = seg_ids[:, :, None] == jnp.arange(seg_total, dtype=jnp.int32)[None, None, :]
    looked_up = jnp.sum(jnp.where(matches, segment_rows[None, None, :], 0), axis=2)
    return jnp.where(valid, looked_up, -1).reshape(-1)


def on_device(
    noisy_state,
    fresh_noise,
    conditioning,
    first_kernel,
    first_bias,
    film_weight,
    film_bias,
    second_kernel,
    second_bias,
    skip_kernel,
    out_kernel,
    strip_table,
    segment_rows,
    step_index,
):
    tile_col = lax.axis_index("gx")
    tile_row = lax.axis_index("gy")
    col_count = lax.axis_size("gx")
    row_count = lax.axis_size("gy")
    channels, tile_rows, tile_cols = noisy_state.shape
    total_rows = tile_rows * row_count
    total_cols = tile_cols * col_count
    spread, scale_in, scale_skip, scale_out, stride = sampler_terms(step_index)
    segs_wide = tile_cols // SEG
    segs_tall = tile_rows // SEG
    slot_count = 2 * (segs_wide + segs_tall)
    wanted = boundary_ids(
        jnp.reshape(tile_col, (1,)),
        jnp.reshape(tile_row, (1,)),
        col_count,
        row_count,
        segs_wide,
        segs_tall,
        segment_rows,
    )
    shard_rows = lax.all_gather(strip_table, "gx", axis=0, tiled=True)
    chosen = (wanted[:, None] == jnp.arange(shard_rows.shape[0], dtype=jnp.int32)[None, :]).astype(
        jnp.bfloat16
    )
    delivered = jnp.dot(chosen, shard_rows, preferred_element_type=jnp.float32)
    table = delivered.reshape(slot_count, channels, BAND, SEG)
    south_side = side_values(table, 0, segs_wide, tile_cols)
    north_side = side_values(table, segs_wide, segs_wide, tile_cols)
    west_side = side_values(table, 2 * segs_wide, segs_tall, tile_rows)
    east_side = side_values(table, 2 * segs_wide + segs_tall, segs_tall, tile_rows)
    state_hat = noisy_state.astype(jnp.float32) + spread * fresh_noise.astype(jnp.float32)
    net_in = jnp.concatenate(
        [scale_in * state_hat, conditioning.astype(jnp.float32)], axis=0
    ).astype(jnp.bfloat16)
    ext = with_halo(net_in)
    pairs_out = residual_block(
        ext,
        first_weights(first_kernel, first_bias, film_weight, film_bias),
        second_weights(second_kernel),
        skip_weights(skip_kernel, second_bias),
        out_weights(out_kernel),
        tile_cols,
    )
    projected = pairs_out.reshape(tile_rows // 2, 2, channels, tile_cols)
    projected = projected.transpose(2, 0, 1, 3).reshape(channels, tile_rows, tile_cols)
    denoised = scale_skip * state_hat + scale_out * projected
    global_rows = (tile_row * tile_rows + jnp.arange(tile_rows, dtype=jnp.int32)).astype(
        jnp.float32
    )
    global_cols = (tile_col * tile_cols + jnp.arange(tile_cols, dtype=jnp.int32)).astype(
        jnp.float32
    )
    south_weight = relax_weight(global_rows, BAND)
    north_weight = relax_weight(total_rows - 1.0 - global_rows, BAND)
    west_weight = relax_weight(global_cols, BAND)
    east_weight = relax_weight(total_cols - 1.0 - global_cols, BAND)
    rest_rows = tile_rows - BAND
    rest_cols = tile_cols - BAND
    south_full = jnp.pad(south_side, ((0, 0), (0, rest_rows), (0, 0)))
    north_full = jnp.pad(north_side[:, ::-1, :], ((0, 0), (rest_rows, 0), (0, 0)))
    west_full = jnp.pad(west_side.transpose(0, 2, 1), ((0, 0), (0, 0), (0, rest_cols)))
    east_full = jnp.pad(east_side.transpose(0, 2, 1)[:, :, ::-1], ((0, 0), (0, 0), (rest_cols, 0)))
    numerator = (
        denoised
        + south_weight[None, :, None] * south_full
        + north_weight[None, :, None] * north_full
    )
    numerator = (
        numerator + west_weight[None, None, :] * west_full + east_weight[None, None, :] * east_full
    )
    denominator = (
        1.0 + south_weight[:, None] + north_weight[:, None] + (west_weight + east_weight)[None, :]
    )
    relaxed = numerator / denominator[None]
    return (state_hat + stride * (state_hat - relaxed)).astype(jnp.bfloat16)


def solution(mesh):
    return jax.shard_map(
        on_device,
        mesh=mesh,
        in_specs=(
            P(None, "gy", "gx"),
            P(None, "gy", "gx"),
            P(None, "gy", "gx"),
            P(),
            P(),
            P(),
            P(),
            P(),
            P(),
            P(),
            P(),
            P("gx", None),
            P(),
            P(),
        ),
        out_specs=P(None, "gy", "gx"),
        check_vma=False,
    )
```

```python
import functools

import jax
import jax.numpy as jnp
from jax import lax
from jax.experimental import pallas as pl
from jax.experimental.pallas import tpu as pltpu
from jax.sharding import PartitionSpec as P

SEG = 32
BAND = 8
NSTEPS = 18


SIGMA_MAX = 800.0
SIGMA_MIN = 0.002
RHO_POWER = 7.0
CHURN_GAIN = 0.25
NOISE_GAIN = 1.007
SIGMA_DATA = 0.5
RELAX_GAIN = 3.0
SUB = 4
ROOT_HALF = 0.7071067811865476


def shifted(block, axis, step):
    count = lax.axis_size(axis)
    if step > 0:
        pairs = [(i, i + 1) for i in range(count - 1)]
    else:
        pairs = [(i + 1, i) for i in range(count - 1)]
    return lax.ppermute(block, axis, pairs)


def halos(net_in):
    channels, rows, cols = net_in.shape
    left = shifted(net_in[:, :, cols - 2 :].transpose(2, 0, 1), "gx", 1)
    right = shifted(net_in[:, :, :2].transpose(2, 0, 1), "gx", -1)
    gap = jnp.zeros((channels, rows, cols - 4), net_in.dtype)
    beside = jnp.concatenate([right.transpose(1, 2, 0), gap, left.transpose(1, 2, 0)], axis=2)
    tail = jnp.concatenate([net_in[:, rows - 2 :], beside[:, rows - 2 :]], axis=2)
    head = jnp.concatenate([net_in[:, :2], beside[:, :2]], axis=2)
    return beside, shifted(tail, "gy", 1), shifted(head, "gy", -1)


def three_parts(values):
    high = lax.reduce_precision(values, 8, 7)
    rest = values - high
    mid = lax.reduce_precision(rest, 8, 7)
    return jnp.stack([high, mid, rest - mid]).astype(jnp.bfloat16)


def bias_rows(values):
    return jnp.pad(three_parts(values), ((0, 13), (0, 0)))


def first_weights(first_kernel, first_bias, film_weight, film_bias):
    width, inner = first_kernel.shape[2], first_kernel.shape[3]
    taps = first_kernel.transpose(1, 0, 3, 2)
    conv = jnp.concatenate(
        [jnp.pad(taps, ((0, 0), (s, 1 - s), (0, 0), (0, 0))) for s in (0, 1)], axis=3
    ).reshape(12 * inner, 2 * width)
    lead = inner - film_weight.shape[1]
    film = jnp.pad(film_weight.T, ((lead, 0), (0, 0)))
    parts = [conv]
    for k in (0, 1):
        piece = film[:, k * width : (k + 1) * width]
        both = jnp.concatenate(
            [jnp.pad(piece, ((inner * (5 + s), inner * (6 - s)), (0, 0))) for s in (0, 1)], axis=1
        )
        parts.append(both)
    parts = [parts[0]] + parts[1:]
    biases = [first_bias, 1.0 + film_bias[:width], film_bias[width:]]
    row = jnp.concatenate([jnp.tile(v, 2) for v in biases])
    return jnp.concatenate([jnp.concatenate(parts, axis=1), bias_rows(row)], axis=0)


def second_weights(second_kernel):
    width, inner = second_kernel.shape[2], second_kernel.shape[3]
    taps = second_kernel.transpose(0, 1, 3, 2).reshape(3, 3 * inner, width)
    return jnp.concatenate(
        [jnp.pad(taps, ((s, 1 - s), (0, 0), (0, 0))) for s in (0, 1)], axis=2
    ).reshape(12 * inner, 2 * width)


def skip_weights(skip_kernel, second_bias):
    width, inner = skip_kernel.shape
    flat = skip_kernel.T
    both = jnp.concatenate(
        [jnp.pad(flat, ((inner * s, inner * (1 - s)), (0, 0))) for s in (0, 1)], axis=1
    )
    return jnp.concatenate([both, bias_rows(jnp.tile(second_bias, 2))], axis=0)


def out_weights(out_kernel):
    width = out_kernel.shape[1]
    return jnp.concatenate(
        [jnp.pad(out_kernel, ((0, 0), (width * s, width * (1 - s)))) for s in (0, 1)], axis=0
    )


def block_kernel(pairs, group, cols, width, main_ref, side_ref, above_ref, below_ref, first_ref,
                 second_ref, out_ref, proj_ref, net_ref, edge_ref, held, patches):
    tile_col, tile_row = lax.axis_index("gx"), lax.axis_index("gy")
    last_col, last_row = lax.axis_size("gx") - 1, lax.axis_size("gy") - 1
    wide = cols + 16
    inner, rows = main_ref.shape[0], main_ref.shape[1]
    for c in range(inner):
        spot = pl.ds(2 * inner + c, rows, stride=inner)
        net_ref[spot] = main_ref[c].astype(jnp.float32)
        edge_ref[spot] = side_ref[c].astype(jnp.float32)
        upper, lower = above_ref[c].astype(jnp.float32), below_ref[c].astype(jnp.float32)
        for r in range(2):
            at, end = r * inner + c, (rows + 2 + r) * inner + c
            net_ref[at : at + 1] = upper[r : r + 1, :cols]
            edge_ref[at : at + 1] = upper[r : r + 1, cols:]
            net_ref[end : end + 1] = lower[r : r + 1, :cols]
            edge_ref[end : end + 1] = lower[r : r + 1, cols:]
    place = lax.broadcasted_iota(jnp.int32, (wide, width), 0)
    low = jnp.where(tile_col == 0, 1, 0)
    high = jnp.where(tile_col == last_col, cols, cols + 1)
    col_mask = ((place >= low) & (place <= high)).astype(jnp.float32)
    ones = jnp.ones((16, wide), jnp.bfloat16)
    depth = 6 * width

    def moved_lanes(x, step):
        return (pltpu.roll(x, step, 1) if step else x).astype(jnp.bfloat16)

    def hidden_pairs(first, count, slot):
        for k in range(count):
            start = pl.multiple_of((first + k) * 32, 32)
            x = jnp.concatenate([net_ref[pl.ds(start, 64)], edge_ref[pl.ds(start, 64)]], axis=1)
            patch = jnp.concatenate([moved_lanes(x, 2 - b)[:, :wide] for b in range(3)] + [ones], axis=0)
            patches[k * wide : (k + 1) * wide] = patch.T
        for top in range(0, count, SUB):
            size = min(SUB, count - top)
            acts = jnp.dot(
                patches[top * wide : (top + size) * wide],
                first_ref[...],
                preferred_element_type=jnp.float32,
            )
            for k in range(size):
                activate(acts[k * wide : (k + 1) * wide], first + top + k, slot + top + k)

    def activate(act, i, slot):
        for s in range(2):
            lo = s * width
            shaped = (
                act[:, lo : lo + width] * act[:, 2 * width + lo : 3 * width + lo]
                + act[:, 4 * width + lo : 5 * width + lo]
            )
            half = 0.5 * shaped
            value = half * jnp.tanh(half) + half
            if s == 0:
                inside = jnp.where((i == 0) & (tile_row == 0), 0.0, 1.0)
            else:
                inside = jnp.where((i == pairs) & (tile_row == last_row), 0.0, 1.0)
            value = value * (col_mask * inside)
            for b in range(3):
                moved = value if b == 0 else pltpu.roll(value, wide - b, 0)
                moved = moved[:cols].astype(jnp.bfloat16)
                at = (s * 3 + b) * width
                held[slot, :, at : at + width] = moved
                if slot > 0:
                    held[slot - 1, :, depth + at : depth + at + width] = moved

    def out_pairs(first):
        for k in range(group):
            start = pl.multiple_of((first + k) * 32 + 32, 32)
            x = net_ref[pl.ds(start, 32)].astype(jnp.bfloat16)
            centre = jnp.concatenate([x, ones[:, :cols]], axis=0)
            held[k, :, 2 * depth :] = centre.T
        total = jnp.dot(
            held[:group].reshape(group * cols, second_ref.shape[0]),
            second_ref[...],
            preferred_element_type=jnp.float32,
        )
        branch = (total * ROOT_HALF).astype(jnp.bfloat16)
        for k in range(group):
            proj_ref[first + k] = lax.dot_general(
                out_ref[...],
                branch[k * cols : (k + 1) * cols],
                (((1,), (1,)), ((), ())),
                preferred_element_type=jnp.float32,
            )

    hidden_pairs(jnp.int32(0), 1, 0)

    @pl.loop(0, pairs // group)
    def _(step):
        hidden_pairs(step * group + 1, group, 1)
        out_pairs(step * group)
        held[0, :, :depth] = held[group, :, :depth]


def residual_block(net_in, beside, above, below, first_w, second_w, skip_w, out_w):
    inner, rows, cols = net_in.shape
    pairs = rows // 2
    width = second_w.shape[1] // 2
    second_w = jnp.concatenate([second_w, skip_w], axis=0)
    wide = cols + 16
    group = 16
    return pl.pallas_call(
        functools.partial(block_kernel, pairs, group, cols, width),
        out_shape=jax.ShapeDtypeStruct((pairs, out_w.shape[0], cols), jnp.float32),
        in_specs=[pl.BlockSpec(memory_space=pltpu.VMEM)] * 7,
        out_specs=pl.BlockSpec(memory_space=pltpu.VMEM),
        scratch_shapes=[
            pltpu.VMEM(((rows + 4) * inner, cols), jnp.float32),
            pltpu.VMEM(((rows + 4) * inner, cols), jnp.float32),
            pltpu.VMEM((group + 1, cols, second_w.shape[0]), jnp.bfloat16),
            pltpu.VMEM((group * wide, first_w.shape[0]), jnp.bfloat16),
        ],
        compiler_params=pltpu.CompilerParams(vmem_limit_bytes=48 * 1024 * 1024),
        cost_estimate=pl.CostEstimate(flops=20_000_000_000, bytes_accessed=8_000_000, transcendentals=4_500_000),
    )(net_in, beside, above, below, first_w, second_w, out_w)


def noise_levels(step_index, total_steps):
    upper_root = SIGMA_MAX ** (1.0 / RHO_POWER)
    lower_root = SIGMA_MIN ** (1.0 / RHO_POWER)
    position = step_index[0].astype(jnp.float32)
    sigma_now = (upper_root + position / (total_steps - 1) * (lower_root - upper_root)) ** RHO_POWER
    sigma_next = (
        upper_root + (position + 1.0) / (total_steps - 1) * (lower_root - upper_root)
    ) ** RHO_POWER
    return (sigma_now, sigma_next)


def sampler_terms(step_index):
    sigma_now, sigma_next = noise_levels(step_index, NSTEPS)
    sigma_hat = (1.0 + CHURN_GAIN) * sigma_now
    spread = NOISE_GAIN * jnp.sqrt(sigma_hat * sigma_hat - sigma_now * sigma_now)
    energy = sigma_hat * sigma_hat + SIGMA_DATA * SIGMA_DATA
    scale_in = 1.0 / jnp.sqrt(energy)
    scale_skip = SIGMA_DATA * SIGMA_DATA / energy
    scale_out = sigma_hat * SIGMA_DATA / jnp.sqrt(energy)
    stride = (sigma_next - sigma_hat) / sigma_hat
    return (spread, scale_in, scale_skip, scale_out, stride)


def relax_weight(distance, band):
    return jnp.where(
        (distance >= 0) & (distance < band), RELAX_GAIN * (band - distance) / band, 0.0
    )


def side_values(table, first_seg, seg_total, length):
    chosen = table[first_seg : first_seg + seg_total]
    return chosen.transpose(1, 2, 0, 3).reshape(table.shape[1], table.shape[2], length)


def boundary_ids(col_ids, row_ids, col_count, row_count, segs_wide, segs_tall, segment_rows):
    seg_total = segment_rows.shape[0]
    along_wide = jnp.arange(segs_wide, dtype=jnp.int32)[None, :]
    along_tall = jnp.arange(segs_tall, dtype=jnp.int32)[None, :]
    wide_all = col_count * segs_wide
    tall_all = row_count * segs_tall
    south_segs = col_ids[:, None] * segs_wide + along_wide
    north_segs = wide_all + col_ids[:, None] * segs_wide + along_wide
    west_segs = 2 * wide_all + row_ids[:, None] * segs_tall + along_tall
    east_segs = 2 * wide_all + tall_all + row_ids[:, None] * segs_tall + along_tall
    seg_ids = jnp.concatenate([south_segs, north_segs, west_segs, east_segs], axis=1)
    valid = jnp.concatenate(
        [
            jnp.broadcast_to((row_ids == 0)[:, None], south_segs.shape),
            jnp.broadcast_to((row_ids == row_count - 1)[:, None], north_segs.shape),
            jnp.broadcast_to((col_ids == 0)[:, None], west_segs.shape),
            jnp.broadcast_to((col_ids == col_count - 1)[:, None], east_segs.shape),
        ],
        axis=1,
    )
    matches = seg_ids[:, :, None] == jnp.arange(seg_total, dtype=jnp.int32)[None, None, :]
    looked_up = jnp.sum(jnp.where(matches, segment_rows[None, None, :], 0), axis=2)
    return jnp.where(valid, looked_up, -1).reshape(-1)


def on_device(
    noisy_state,
    fresh_noise,
    conditioning,
    first_kernel,
    first_bias,
    film_weight,
    film_bias,
    second_kernel,
    second_bias,
    skip_kernel,
    out_kernel,
    strip_table,
    segment_rows,
    step_index,
):
    tile_col = lax.axis_index("gx")
    tile_row = lax.axis_index("gy")
    col_count = lax.axis_size("gx")
    row_count = lax.axis_size("gy")
    channels, tile_rows, tile_cols = noisy_state.shape
    total_rows = tile_rows * row_count
    total_cols = tile_cols * col_count
    spread, scale_in, scale_skip, scale_out, stride = sampler_terms(step_index)
    segs_wide = tile_cols // SEG
    segs_tall = tile_rows // SEG
    slot_count = 2 * (segs_wide + segs_tall)
    wanted = boundary_ids(
        jnp.reshape(tile_col, (1,)),
        jnp.reshape(tile_row, (1,)),
        col_count,
        row_count,
        segs_wide,
        segs_tall,
        segment_rows,
    )
    shard_rows = lax.all_gather(strip_table, "gx", axis=0, tiled=True)
    chosen = (wanted[:, None] == jnp.arange(shard_rows.shape[0], dtype=jnp.int32)[None, :]).astype(
        jnp.bfloat16
    )
    delivered = jnp.dot(chosen, shard_rows, preferred_element_type=jnp.float32)
    table = delivered.reshape(slot_count, channels, BAND, SEG)
    south_side = side_values(table, 0, segs_wide, tile_cols)
    north_side = side_values(table, segs_wide, segs_wide, tile_cols)
    west_side = side_values(table, 2 * segs_wide, segs_tall, tile_rows)
    east_side = side_values(table, 2 * segs_wide + segs_tall, segs_tall, tile_rows)
    state_hat = noisy_state.astype(jnp.float32) + spread * fresh_noise.astype(jnp.float32)
    net_in = jnp.concatenate(
        [scale_in * state_hat, conditioning.astype(jnp.float32)], axis=0
    ).astype(jnp.bfloat16)
    pairs_out = residual_block(
        net_in,
        *halos(net_in),
        first_weights(first_kernel, first_bias, film_weight, film_bias),
        second_weights(second_kernel),
        skip_weights(skip_kernel, second_bias),
        out_weights(out_kernel),
    )
    projected = pairs_out.reshape(tile_rows // 2, 2, channels, tile_cols)
    projected = projected.transpose(2, 0, 1, 3).reshape(channels, tile_rows, tile_cols)
    denoised = scale_skip * state_hat + scale_out * projected
    global_rows = (tile_row * tile_rows + jnp.arange(tile_rows, dtype=jnp.int32)).astype(
        jnp.float32
    )
    global_cols = (tile_col * tile_cols + jnp.arange(tile_cols, dtype=jnp.int32)).astype(
        jnp.float32
    )
    south_weight = relax_weight(global_rows, BAND)
    north_weight = relax_weight(total_rows - 1.0 - global_rows, BAND)
    west_weight = relax_weight(global_cols, BAND)
    east_weight = relax_weight(total_cols - 1.0 - global_cols, BAND)
    rest_rows = tile_rows - BAND
    rest_cols = tile_cols - BAND
    south_full = jnp.pad(south_side, ((0, 0), (0, rest_rows), (0, 0)))
    north_full = jnp.pad(north_side[:, ::-1, :], ((0, 0), (rest_rows, 0), (0, 0)))
    west_full = jnp.pad(west_side.transpose(0, 2, 1), ((0, 0), (0, 0), (0, rest_cols)))
    east_full = jnp.pad(east_side.transpose(0, 2, 1)[:, :, ::-1], ((0, 0), (0, 0), (rest_cols, 0)))
    numerator = (
        denoised
        + south_weight[None, :, None] * south_full
        + north_weight[None, :, None] * north_full
    )
    numerator = (
        numerator + west_weight[None, None, :] * west_full + east_weight[None, None, :] * east_full
    )
    denominator = (
        1.0 + south_weight[:, None] + north_weight[:, None] + (west_weight + east_weight)[None, :]
    )
    relaxed = numerator / denominator[None]
    return (state_hat + stride * (state_hat - relaxed)).astype(jnp.bfloat16)


def solution(mesh):
    return jax.shard_map(
        on_device,
        mesh=mesh,
        in_specs=(
            P(None, "gy", "gx"),
            P(None, "gy", "gx"),
            P(None, "gy", "gx"),
            P(),
            P(),
            P(),
            P(),
            P(),
            P(),
            P(),
            P(),
            P("gx", None),
            P(),
            P(),
        ),
        out_specs=P(None, "gy", "gx"),
        check_vma=False,
    )
```

```python
import functools

import jax
import jax.numpy as jnp
from jax import lax
from jax.experimental import pallas as pl
from jax.experimental.pallas import tpu as pltpu
from jax.sharding import PartitionSpec as P

SEG = 32
BAND = 8
NSTEPS = 18


SIGMA_MAX = 800.0
SIGMA_MIN = 0.002
RHO_POWER = 7.0
CHURN_GAIN = 0.25
NOISE_GAIN = 1.007
SIGMA_DATA = 0.5
RELAX_GAIN = 3.0
SUB = 4
ROOT_HALF = 0.7071067811865476


def shifted(block, axis, step):
    count = lax.axis_size(axis)
    if step > 0:
        pairs = [(i, i + 1) for i in range(count - 1)]
    else:
        pairs = [(i + 1, i) for i in range(count - 1)]
    return lax.ppermute(block, axis, pairs)


def halos(net_in):
    channels, rows, cols = net_in.shape
    left = shifted(net_in[:, :, cols - 2 :].transpose(2, 0, 1), "gx", 1)
    right = shifted(net_in[:, :, :2].transpose(2, 0, 1), "gx", -1)
    gap = jnp.zeros((channels, rows, cols - 4), net_in.dtype)
    beside = jnp.concatenate([right.transpose(1, 2, 0), gap, left.transpose(1, 2, 0)], axis=2)
    tail = jnp.concatenate([net_in[:, rows - 2 :], beside[:, rows - 2 :]], axis=2)
    head = jnp.concatenate([net_in[:, :2], beside[:, :2]], axis=2)
    return beside, shifted(tail, "gy", 1), shifted(head, "gy", -1)


def three_parts(values):
    high = lax.reduce_precision(values, 8, 7)
    rest = values - high
    mid = lax.reduce_precision(rest, 8, 7)
    return jnp.stack([high, mid, rest - mid]).astype(jnp.bfloat16)


def bias_rows(values):
    return jnp.pad(three_parts(values), ((0, 13), (0, 0)))


def first_weights(first_kernel, first_bias, film_weight, film_bias):
    width, inner = first_kernel.shape[2], first_kernel.shape[3]
    taps = first_kernel.transpose(1, 0, 3, 2)
    conv = jnp.concatenate(
        [jnp.pad(taps, ((0, 0), (s, 1 - s), (0, 0), (0, 0))) for s in (0, 1)], axis=3
    ).reshape(12 * inner, 2 * width)
    lead = inner - film_weight.shape[1]
    film = jnp.pad(film_weight.T, ((lead, 0), (0, 0)))
    parts = [conv]
    for k in (0, 1):
        piece = film[:, k * width : (k + 1) * width]
        both = jnp.concatenate(
            [jnp.pad(piece, ((inner * (5 + s), inner * (6 - s)), (0, 0))) for s in (0, 1)], axis=1
        )
        parts.append(both)
    parts = [parts[0]] + parts[1:]
    biases = [first_bias, 1.0 + film_bias[:width], film_bias[width:]]
    row = jnp.concatenate([jnp.tile(v, 2) for v in biases])
    return jnp.concatenate([jnp.concatenate(parts, axis=1), bias_rows(row)], axis=0)


def second_weights(second_kernel):
    width, inner = second_kernel.shape[2], second_kernel.shape[3]
    taps = second_kernel.transpose(0, 1, 3, 2).reshape(3, 3 * inner, width)
    return jnp.concatenate(
        [jnp.pad(taps, ((s, 1 - s), (0, 0), (0, 0))) for s in (0, 1)], axis=2
    ).reshape(12 * inner, 2 * width)


def skip_weights(skip_kernel, second_bias):
    width, inner = skip_kernel.shape
    flat = skip_kernel.T
    both = jnp.concatenate(
        [jnp.pad(flat, ((inner * s, inner * (1 - s)), (0, 0))) for s in (0, 1)], axis=1
    )
    return jnp.concatenate([both, bias_rows(jnp.tile(second_bias, 2))], axis=0)


def out_weights(out_kernel):
    width = out_kernel.shape[1]
    return jnp.concatenate(
        [jnp.pad(out_kernel, ((0, 0), (width * s, width * (1 - s)))) for s in (0, 1)], axis=0
    )


def block_kernel(pairs, group, cols, width, main_ref, side_ref, above_ref, below_ref, first_ref,
                 second_ref, out_ref, proj_ref, net_ref, edge_ref, held, patches):
    tile_col, tile_row = lax.axis_index("gx"), lax.axis_index("gy")
    last_col, last_row = lax.axis_size("gx") - 1, lax.axis_size("gy") - 1
    wide = cols + 16
    inner, rows = main_ref.shape[0], main_ref.shape[1]
    for c in range(inner):
        spot = pl.ds(2 * inner + c, rows, stride=inner)
        net_ref[spot] = main_ref[c].astype(jnp.float32)
        edge_ref[spot] = side_ref[c].astype(jnp.float32)
        upper, lower = above_ref[c].astype(jnp.float32), below_ref[c].astype(jnp.float32)
        for r in range(2):
            at, end = r * inner + c, (rows + 2 + r) * inner + c
            net_ref[at : at + 1] = upper[r : r + 1, :cols]
            edge_ref[at : at + 1] = upper[r : r + 1, cols:]
            net_ref[end : end + 1] = lower[r : r + 1, :cols]
            edge_ref[end : end + 1] = lower[r : r + 1, cols:]
    place = lax.broadcasted_iota(jnp.int32, (wide, width), 0)
    low = jnp.where(tile_col == 0, 1, 0)
    high = jnp.where(tile_col == last_col, cols, cols + 1)
    col_mask = ((place >= low) & (place <= high)).astype(jnp.float32)
    ones = jnp.ones((16, wide), jnp.bfloat16)
    depth = 6 * width

    def moved_lanes(x, step):
        return (pltpu.roll(x, step, 1) if step else x).astype(jnp.bfloat16)

    def hidden_pairs(first, count, slot):
        for k in range(count):
            start = pl.multiple_of((first + k) * 32, 32)
            x = jnp.concatenate([net_ref[pl.ds(start, 64)], edge_ref[pl.ds(start, 64)]], axis=1)
            patch = jnp.concatenate([moved_lanes(x, 2 - b)[:, :wide] for b in range(3)] + [ones], axis=0)
            patches[k * wide : (k + 1) * wide] = patch.T
        for top in range(0, count, SUB):
            size = min(SUB, count - top)
            acts = jnp.dot(
                patches[top * wide : (top + size) * wide],
                first_ref[...],
                preferred_element_type=jnp.float32,
            )
            for k in range(size):
                activate(acts[k * wide : (k + 1) * wide], first + top + k, slot + top + k)

    def activate(act, i, slot):
        for s in range(2):
            lo = s * width
            shaped = (
                act[:, lo : lo + width] * act[:, 2 * width + lo : 3 * width + lo]
                + act[:, 4 * width + lo : 5 * width + lo]
            )
            half = 0.5 * shaped
            value = half * jnp.tanh(half) + half
            if s == 0:
                inside = jnp.where((i == 0) & (tile_row == 0), 0.0, 1.0)
            else:
                inside = jnp.where((i == pairs) & (tile_row == last_row), 0.0, 1.0)
            value = value * (col_mask * inside)
            for b in range(3):
                moved = value if b == 0 else pltpu.roll(value, wide - b, 0)
                moved = moved[:cols].astype(jnp.bfloat16)
                at = (s * 3 + b) * width
                held[slot, :, at : at + width] = moved
                if slot > 0:
                    held[slot - 1, :, depth + at : depth + at + width] = moved

    def out_pairs(first):
        for k in range(group):
            start = pl.multiple_of((first + k) * 32 + 32, 32)
            x = net_ref[pl.ds(start, 32)].astype(jnp.bfloat16)
            centre = jnp.concatenate([x, ones[:, :cols]], axis=0)
            held[k, :, 2 * depth :] = centre.T
        total = jnp.dot(
            held[:group].reshape(group * cols, second_ref.shape[0]),
            second_ref[...],
            preferred_element_type=jnp.float32,
        )
        branch = (total * ROOT_HALF).astype(jnp.bfloat16)
        for k in range(group):
            proj_ref[first + k] = lax.dot_general(
                out_ref[...],
                branch[k * cols : (k + 1) * cols],
                (((1,), (1,)), ((), ())),
                preferred_element_type=jnp.float32,
            )

    hidden_pairs(jnp.int32(0), 1, 0)

    @pl.loop(0, pairs // group)
    def _(step):
        hidden_pairs(step * group + 1, group, 1)
        out_pairs(step * group)
        held[0, :, :depth] = held[group, :, :depth]


def residual_block(net_in, beside, above, below, first_w, second_w, skip_w, out_w):
    inner, rows, cols = net_in.shape
    pairs = rows // 2
    width = second_w.shape[1] // 2
    second_w = jnp.concatenate([second_w, skip_w], axis=0)
    wide = cols + 16
    group = 16
    return pl.pallas_call(
        functools.partial(block_kernel, pairs, group, cols, width),
        out_shape=jax.ShapeDtypeStruct((pairs, out_w.shape[0], cols), jnp.float32),
        in_specs=[pl.BlockSpec(memory_space=pltpu.VMEM)] * 7,
        out_specs=pl.BlockSpec(memory_space=pltpu.VMEM),
        scratch_shapes=[
            pltpu.VMEM(((rows + 4) * inner, cols), jnp.float32),
            pltpu.VMEM(((rows + 4) * inner, cols), jnp.float32),
            pltpu.VMEM((group + 1, cols, second_w.shape[0]), jnp.bfloat16),
            pltpu.VMEM((group * wide, first_w.shape[0]), jnp.bfloat16),
        ],
        compiler_params=pltpu.CompilerParams(vmem_limit_bytes=48 * 1024 * 1024),
        cost_estimate=pl.CostEstimate(flops=20_000_000_000, bytes_accessed=8_000_000, transcendentals=4_500_000),
    )(net_in, beside, above, below, first_w, second_w, out_w)


def noise_levels(step_index, total_steps):
    upper_root = SIGMA_MAX ** (1.0 / RHO_POWER)
    lower_root = SIGMA_MIN ** (1.0 / RHO_POWER)
    position = step_index[0].astype(jnp.float32)
    sigma_now = (upper_root + position / (total_steps - 1) * (lower_root - upper_root)) ** RHO_POWER
    sigma_next = (
        upper_root + (position + 1.0) / (total_steps - 1) * (lower_root - upper_root)
    ) ** RHO_POWER
    return (sigma_now, sigma_next)


def sampler_terms(step_index):
    sigma_now, sigma_next = noise_levels(step_index, NSTEPS)
    sigma_hat = (1.0 + CHURN_GAIN) * sigma_now
    spread = NOISE_GAIN * jnp.sqrt(sigma_hat * sigma_hat - sigma_now * sigma_now)
    energy = sigma_hat * sigma_hat + SIGMA_DATA * SIGMA_DATA
    scale_in = 1.0 / jnp.sqrt(energy)
    scale_skip = SIGMA_DATA * SIGMA_DATA / energy
    scale_out = sigma_hat * SIGMA_DATA / jnp.sqrt(energy)
    stride = (sigma_next - sigma_hat) / sigma_hat
    return (spread, scale_in, scale_skip, scale_out, stride)


def relax_weight(distance, band):
    return jnp.where(
        (distance >= 0) & (distance < band), RELAX_GAIN * (band - distance) / band, 0.0
    )


def boundary_ids(col_ids, row_ids, col_count, row_count, segs_wide, segs_tall, segment_rows):
    seg_total = segment_rows.shape[0]
    along_wide = jnp.arange(segs_wide, dtype=jnp.int32)[None, :]
    along_tall = jnp.arange(segs_tall, dtype=jnp.int32)[None, :]
    wide_all = col_count * segs_wide
    tall_all = row_count * segs_tall
    south_segs = col_ids[:, None] * segs_wide + along_wide
    north_segs = wide_all + col_ids[:, None] * segs_wide + along_wide
    west_segs = 2 * wide_all + row_ids[:, None] * segs_tall + along_tall
    east_segs = 2 * wide_all + tall_all + row_ids[:, None] * segs_tall + along_tall
    seg_ids = jnp.concatenate([south_segs, north_segs, west_segs, east_segs], axis=1)
    valid = jnp.concatenate(
        [
            jnp.broadcast_to((row_ids == 0)[:, None], south_segs.shape),
            jnp.broadcast_to((row_ids == row_count - 1)[:, None], north_segs.shape),
            jnp.broadcast_to((col_ids == 0)[:, None], west_segs.shape),
            jnp.broadcast_to((col_ids == col_count - 1)[:, None], east_segs.shape),
        ],
        axis=1,
    )
    matches = seg_ids[:, :, None] == jnp.arange(seg_total, dtype=jnp.int32)[None, None, :]
    looked_up = jnp.sum(jnp.where(matches, segment_rows[None, None, :], 0), axis=2)
    return jnp.where(valid, looked_up, -1).reshape(-1)


def on_device(
    noisy_state,
    fresh_noise,
    conditioning,
    first_kernel,
    first_bias,
    film_weight,
    film_bias,
    second_kernel,
    second_bias,
    skip_kernel,
    out_kernel,
    strip_table,
    segment_rows,
    step_index,
):
    tile_col = lax.axis_index("gx")
    tile_row = lax.axis_index("gy")
    col_count = lax.axis_size("gx")
    row_count = lax.axis_size("gy")
    channels, tile_rows, tile_cols = noisy_state.shape
    total_rows = tile_rows * row_count
    total_cols = tile_cols * col_count
    spread, scale_in, scale_skip, scale_out, stride = sampler_terms(step_index)
    segs_wide = tile_cols // SEG
    segs_tall = tile_rows // SEG
    slot_count = 2 * (segs_wide + segs_tall)
    wanted = boundary_ids(
        jnp.reshape(tile_col, (1,)),
        jnp.reshape(tile_row, (1,)),
        col_count,
        row_count,
        segs_wide,
        segs_tall,
        segment_rows,
    )
    shard_rows = lax.all_gather(strip_table, "gx", axis=0, tiled=True)
    chosen = (wanted[:, None] == jnp.arange(shard_rows.shape[0], dtype=jnp.int32)[None, :]).astype(
        jnp.bfloat16
    )
    delivered = jnp.dot(chosen, shard_rows, preferred_element_type=jnp.float32)
    table = delivered.astype(jnp.bfloat16).reshape(slot_count, channels * BAND, SEG)
    table = table.transpose(1, 0, 2).reshape(channels, BAND, slot_count * SEG)
    south_side, north_side = table[:, :, :tile_cols], table[:, :, tile_cols : 2 * tile_cols]
    west_side = table[:, :, 2 * tile_cols : 2 * tile_cols + tile_rows]
    east_side = table[:, :, 2 * tile_cols + tile_rows :]
    state_hat = noisy_state.astype(jnp.float32) + spread * fresh_noise.astype(jnp.float32)
    net_in = jnp.concatenate(
        [scale_in * state_hat, conditioning.astype(jnp.float32)], axis=0
    ).astype(jnp.bfloat16)
    pairs_out = residual_block(
        net_in,
        *halos(net_in),
        first_weights(first_kernel, first_bias, film_weight, film_bias),
        second_weights(second_kernel),
        skip_weights(skip_kernel, second_bias),
        out_weights(out_kernel),
    )
    projected = pairs_out.reshape(tile_rows // 2, 2, channels, tile_cols)
    projected = projected.transpose(2, 0, 1, 3).reshape(channels, tile_rows, tile_cols)
    denoised = scale_skip * state_hat + scale_out * projected
    global_rows = (tile_row * tile_rows + jnp.arange(tile_rows, dtype=jnp.int32)).astype(
        jnp.float32
    )
    global_cols = (tile_col * tile_cols + jnp.arange(tile_cols, dtype=jnp.int32)).astype(
        jnp.float32
    )
    south_weight = relax_weight(global_rows, BAND)
    north_weight = relax_weight(total_rows - 1.0 - global_rows, BAND)
    west_weight = relax_weight(global_cols, BAND)
    east_weight = relax_weight(total_cols - 1.0 - global_cols, BAND)
    depths = jnp.arange(BAND, dtype=jnp.float32)[:, None]

    def placed(weight, distance):
        return jnp.where(distance[None, :] == depths, weight[None, :], 0.0).astype(jnp.bfloat16)

    by_row = jnp.concatenate(
        [
            placed(south_weight, global_rows),
            placed(north_weight, total_rows - 1.0 - global_rows),
        ],
        axis=0,
    )
    by_col = jnp.concatenate(
        [
            placed(west_weight, global_cols),
            placed(east_weight, total_cols - 1.0 - global_cols),
        ],
        axis=0,
    )
    every = (channels, 2 * BAND)
    along_rows = jnp.concatenate(
        [jnp.broadcast_to(by_row, every + by_row.shape[1:]), west_side, east_side], axis=1
    )
    along_cols = jnp.concatenate(
        [south_side, north_side, jnp.broadcast_to(by_col, every + by_col.shape[1:])], axis=1
    )
    targets = jnp.einsum("ckh,ckw->chw", along_rows, along_cols, preferred_element_type=jnp.float32)
    numerator = denoised + targets
    denominator = (
        1.0 + south_weight[:, None] + north_weight[:, None] + (west_weight + east_weight)[None, :]
    )
    relaxed = numerator / denominator[None]
    return (state_hat + stride * (state_hat - relaxed)).astype(jnp.bfloat16)


def solution(mesh):
    return jax.shard_map(
        on_device,
        mesh=mesh,
        in_specs=(
            P(None, "gy", "gx"),
            P(None, "gy", "gx"),
            P(None, "gy", "gx"),
            P(),
            P(),
            P(),
            P(),
            P(),
            P(),
            P(),
            P(),
            P("gx", None),
            P(),
            P(),
        ),
        out_specs=P(None, "gy", "gx"),
        check_vma=False,
    )
```

```python
import functools

import jax
import jax.numpy as jnp
from jax import lax
from jax.experimental import pallas as pl
from jax.experimental.pallas import tpu as pltpu
from jax.sharding import PartitionSpec as P

SEG = 32
BAND = 8
NSTEPS = 18


SIGMA_MAX = 800.0
SIGMA_MIN = 0.002
RHO_POWER = 7.0
CHURN_GAIN = 0.25
NOISE_GAIN = 1.007
SIGMA_DATA = 0.5
RELAX_GAIN = 3.0
SUB = 1
ROOT_HALF = 0.7071067811865476


def shifted(block, axis, step):
    count = lax.axis_size(axis)
    if step > 0:
        pairs = [(i, i + 1) for i in range(count - 1)]
    else:
        pairs = [(i + 1, i) for i in range(count - 1)]
    return lax.ppermute(block, axis, pairs)


def halos(net_in):
    channels, rows, cols = net_in.shape
    left = shifted(net_in[:, :, cols - 2 :].transpose(2, 0, 1), "gx", 1)
    right = shifted(net_in[:, :, :2].transpose(2, 0, 1), "gx", -1)
    gap = jnp.zeros((channels, 2, cols - 4), net_in.dtype)

    def whole(top):
        ends = [side[:, :, top : top + 2].transpose(1, 2, 0) for side in (right, left)]
        return jnp.concatenate([net_in[:, top : top + 2], ends[0], gap, ends[1]], axis=2)

    return left, right, shifted(whole(rows - 2), "gy", 1), shifted(whole(0), "gy", -1)


def three_parts(values):
    high = lax.reduce_precision(values, 8, 7)
    rest = values - high
    mid = lax.reduce_precision(rest, 8, 7)
    return jnp.stack([high, mid, rest - mid]).astype(jnp.bfloat16)


def bias_rows(values):
    return jnp.pad(three_parts(values), ((0, 13), (0, 0)))


def first_weights(first_kernel, first_bias, film_weight, film_bias):
    width, inner = first_kernel.shape[2], first_kernel.shape[3]
    taps = first_kernel.transpose(1, 0, 3, 2)
    conv = jnp.concatenate(
        [jnp.pad(taps, ((0, 0), (s, 1 - s), (0, 0), (0, 0))) for s in (0, 1)], axis=3
    ).reshape(12 * inner, 2 * width)
    lead = inner - film_weight.shape[1]
    film = jnp.pad(film_weight.T, ((lead, 0), (0, 0)))
    parts = [conv]
    for k in (0, 1):
        piece = film[:, k * width : (k + 1) * width]
        both = jnp.concatenate(
            [jnp.pad(piece, ((inner * (5 + s), inner * (6 - s)), (0, 0))) for s in (0, 1)], axis=1
        )
        parts.append(both)
    parts = [parts[0]] + parts[1:]
    biases = [first_bias, 1.0 + film_bias[:width], film_bias[width:]]
    row = jnp.concatenate([jnp.tile(v, 2) for v in biases])
    return jnp.concatenate([jnp.concatenate(parts, axis=1), bias_rows(row)], axis=0)


def second_weights(second_kernel):
    width, inner = second_kernel.shape[2], second_kernel.shape[3]
    taps = second_kernel.transpose(0, 1, 3, 2).reshape(3, 3 * inner, width)
    return jnp.concatenate(
        [jnp.pad(taps, ((s, 1 - s), (0, 0), (0, 0))) for s in (0, 1)], axis=2
    ).reshape(12 * inner, 2 * width)


def skip_weights(skip_kernel, second_bias):
    width, inner = skip_kernel.shape
    flat = skip_kernel.T
    both = jnp.concatenate(
        [jnp.pad(flat, ((inner * s, inner * (1 - s)), (0, 0))) for s in (0, 1)], axis=1
    )
    return jnp.concatenate([both, bias_rows(jnp.tile(second_bias, 2))], axis=0)


def out_weights(out_kernel):
    width = out_kernel.shape[1]
    return jnp.concatenate(
        [jnp.pad(out_kernel, ((0, 0), (width * s, width * (1 - s)))) for s in (0, 1)], axis=0
    )


def block_kernel(pairs, group, cols, width, main_ref, left_ref, right_ref, above_ref, below_ref,
                 first_ref, second_ref, out_ref, proj_ref, net_ref, edge_ref, held, patches):
    tile_col, tile_row = lax.axis_index("gx"), lax.axis_index("gy")
    last_col, last_row = lax.axis_size("gx") - 1, lax.axis_size("gy") - 1
    wide = cols + 16
    inner, rows = main_ref.shape[0], main_ref.shape[1]
    gap = jnp.zeros((cols - 4, rows), jnp.float32)
    for c in range(inner):
        spot = pl.ds(2 * inner + c, rows, stride=inner)
        net_ref[spot] = main_ref[c].astype(jnp.float32)
        beside = jnp.concatenate(
            [right_ref[:, c].astype(jnp.float32), gap, left_ref[:, c].astype(jnp.float32)], axis=0
        )
        edge_ref[spot] = beside.T
        upper, lower = above_ref[c].astype(jnp.float32), below_ref[c].astype(jnp.float32)
        for r in range(2):
            at, end = r * inner + c, (rows + 2 + r) * inner + c
            net_ref[at : at + 1] = upper[r : r + 1, :cols]
            edge_ref[at : at + 1] = upper[r : r + 1, cols:]
            net_ref[end : end + 1] = lower[r : r + 1, :cols]
            edge_ref[end : end + 1] = lower[r : r + 1, cols:]
    place = lax.broadcasted_iota(jnp.int32, (wide, width), 0)
    low = jnp.where(tile_col == 0, 1, 0)
    high = jnp.where(tile_col == last_col, cols, cols + 1)
    col_mask = ((place >= low) & (place <= high)).astype(jnp.float32)
    ones = jnp.ones((16, wide), jnp.bfloat16)
    depth = 6 * width

    def moved_lanes(x, step):
        return (pltpu.roll(x, step, 1) if step else x).astype(jnp.bfloat16)

    def hidden_pairs(first, count, slot):
        for k in range(count):
            start = pl.multiple_of((first + k) * 32, 32)
            x = jnp.concatenate([net_ref[pl.ds(start, 64)], edge_ref[pl.ds(start, 64)]], axis=1)
            patch = jnp.concatenate([moved_lanes(x, 2 - b)[:, :wide] for b in range(3)] + [ones], axis=0)
            patches[k * wide : (k + 1) * wide] = patch.T
        for top in range(0, count, SUB):
            size = min(SUB, count - top)
            acts = jnp.dot(
                patches[top * wide : (top + size) * wide],
                first_ref[...],
                preferred_element_type=jnp.float32,
            )
            for k in range(size):
                activate(acts[k * wide : (k + 1) * wide], first + top + k, slot + top + k)

    def activate(act, i, slot):
        for s in range(2):
            lo = s * width
            shaped = (
                act[:, lo : lo + width] * act[:, 2 * width + lo : 3 * width + lo]
                + act[:, 4 * width + lo : 5 * width + lo]
            )
            half = 0.5 * shaped
            value = half * jnp.tanh(half) + half
            if s == 0:
                inside = jnp.where((i == 0) & (tile_row == 0), 0.0, 1.0)
            else:
                inside = jnp.where((i == pairs) & (tile_row == last_row), 0.0, 1.0)
            value = value * (col_mask * inside)
            for b in range(3):
                moved = value if b == 0 else pltpu.roll(value, wide - b, 0)
                moved = moved[:cols].astype(jnp.bfloat16)
                at = (s * 3 + b) * width
                held[slot, :, at : at + width] = moved
                if slot > 0:
                    held[slot - 1, :, depth + at : depth + at + width] = moved

    def out_pairs(first):
        for k in range(group):
            start = pl.multiple_of((first + k) * 32 + 32, 32)
            x = net_ref[pl.ds(start, 32)].astype(jnp.bfloat16)
            centre = jnp.concatenate([x, ones[:, :cols]], axis=0)
            held[k, :, 2 * depth :] = centre.T
        total = jnp.dot(
            held[:group].reshape(group * cols, second_ref.shape[0]),
            second_ref[...],
            preferred_element_type=jnp.float32,
        )
        branch = (total * ROOT_HALF).astype(jnp.bfloat16)
        for k in range(group):
            proj_ref[first + k] = lax.dot_general(
                out_ref[...],
                branch[k * cols : (k + 1) * cols],
                (((1,), (1,)), ((), ())),
                preferred_element_type=jnp.float32,
            )

    hidden_pairs(jnp.int32(0), 1, 0)

    @pl.loop(0, pairs // group)
    def _(step):
        hidden_pairs(step * group + 1, group, 1)
        out_pairs(step * group)
        held[0, :, :depth] = held[group, :, :depth]


def residual_block(net_in, left, right, above, below, first_w, second_w, skip_w, out_w):
    inner, rows, cols = net_in.shape
    pairs = rows // 2
    width = second_w.shape[1] // 2
    second_w = jnp.concatenate([second_w, skip_w], axis=0)
    wide = cols + 16
    group = 16
    return pl.pallas_call(
        functools.partial(block_kernel, pairs, group, cols, width),
        out_shape=jax.ShapeDtypeStruct((pairs, out_w.shape[0], cols), jnp.float32),
        in_specs=[pl.BlockSpec(memory_space=pltpu.VMEM)] * 8,
        out_specs=pl.BlockSpec(memory_space=pltpu.VMEM),
        scratch_shapes=[
            pltpu.VMEM(((rows + 4) * inner, cols), jnp.float32),
            pltpu.VMEM(((rows + 4) * inner, cols), jnp.float32),
            pltpu.VMEM((group + 1, cols, second_w.shape[0]), jnp.bfloat16),
            pltpu.VMEM((group * wide, first_w.shape[0]), jnp.bfloat16),
        ],
        compiler_params=pltpu.CompilerParams(vmem_limit_bytes=48 * 1024 * 1024),
        cost_estimate=pl.CostEstimate(flops=20_000_000_000, bytes_accessed=8_000_000, transcendentals=4_500_000),
    )(net_in, left, right, above, below, first_w, second_w, out_w)


def noise_levels(step_index, total_steps):
    upper_root = SIGMA_MAX ** (1.0 / RHO_POWER)
    lower_root = SIGMA_MIN ** (1.0 / RHO_POWER)
    position = step_index[0].astype(jnp.float32)
    sigma_now = (upper_root + position / (total_steps - 1) * (lower_root - upper_root)) ** RHO_POWER
    sigma_next = (
        upper_root + (position + 1.0) / (total_steps - 1) * (lower_root - upper_root)
    ) ** RHO_POWER
    return (sigma_now, sigma_next)


def sampler_terms(step_index):
    sigma_now, sigma_next = noise_levels(step_index, NSTEPS)
    sigma_hat = (1.0 + CHURN_GAIN) * sigma_now
    spread = NOISE_GAIN * jnp.sqrt(sigma_hat * sigma_hat - sigma_now * sigma_now)
    energy = sigma_hat * sigma_hat + SIGMA_DATA * SIGMA_DATA
    scale_in = 1.0 / jnp.sqrt(energy)
    scale_skip = SIGMA_DATA * SIGMA_DATA / energy
    scale_out = sigma_hat * SIGMA_DATA / jnp.sqrt(energy)
    stride = (sigma_next - sigma_hat) / sigma_hat
    return (spread, scale_in, scale_skip, scale_out, stride)


def relax_weight(distance, band):
    return jnp.where(
        (distance >= 0) & (distance < band), RELAX_GAIN * (band - distance) / band, 0.0
    )


def boundary_ids(col_ids, row_ids, col_count, row_count, segs_wide, segs_tall, segment_rows):
    seg_total = segment_rows.shape[0]
    along_wide = jnp.arange(segs_wide, dtype=jnp.int32)[None, :]
    along_tall = jnp.arange(segs_tall, dtype=jnp.int32)[None, :]
    wide_all = col_count * segs_wide
    tall_all = row_count * segs_tall
    south_segs = col_ids[:, None] * segs_wide + along_wide
    north_segs = wide_all + col_ids[:, None] * segs_wide + along_wide
    west_segs = 2 * wide_all + row_ids[:, None] * segs_tall + along_tall
    east_segs = 2 * wide_all + tall_all + row_ids[:, None] * segs_tall + along_tall
    seg_ids = jnp.concatenate([south_segs, north_segs, west_segs, east_segs], axis=1)
    valid = jnp.concatenate(
        [
            jnp.broadcast_to((row_ids == 0)[:, None], south_segs.shape),
            jnp.broadcast_to((row_ids == row_count - 1)[:, None], north_segs.shape),
            jnp.broadcast_to((col_ids == 0)[:, None], west_segs.shape),
            jnp.broadcast_to((col_ids == col_count - 1)[:, None], east_segs.shape),
        ],
        axis=1,
    )
    matches = seg_ids[:, :, None] == jnp.arange(seg_total, dtype=jnp.int32)[None, None, :]
    looked_up = jnp.sum(jnp.where(matches, segment_rows[None, None, :], 0), axis=2)
    return jnp.where(valid, looked_up, -1).reshape(-1)


def on_device(
    noisy_state,
    fresh_noise,
    conditioning,
    first_kernel,
    first_bias,
    film_weight,
    film_bias,
    second_kernel,
    second_bias,
    skip_kernel,
    out_kernel,
    strip_table,
    segment_rows,
    step_index,
):
    tile_col = lax.axis_index("gx")
    tile_row = lax.axis_index("gy")
    col_count = lax.axis_size("gx")
    row_count = lax.axis_size("gy")
    channels, tile_rows, tile_cols = noisy_state.shape
    total_rows = tile_rows * row_count
    total_cols = tile_cols * col_count
    spread, scale_in, scale_skip, scale_out, stride = sampler_terms(step_index)
    segs_wide = tile_cols // SEG
    segs_tall = tile_rows // SEG
    slot_count = 2 * (segs_wide + segs_tall)
    wanted = boundary_ids(
        jnp.reshape(tile_col, (1,)),
        jnp.reshape(tile_row, (1,)),
        col_count,
        row_count,
        segs_wide,
        segs_tall,
        segment_rows,
    )
    shard_rows = lax.all_gather(strip_table, "gx", axis=0, tiled=True)
    chosen = (wanted[:, None] == jnp.arange(shard_rows.shape[0], dtype=jnp.int32)[None, :]).astype(
        jnp.bfloat16
    )
    delivered = jnp.dot(chosen, shard_rows, preferred_element_type=jnp.float32)
    table = delivered.astype(jnp.bfloat16).reshape(slot_count, channels * BAND, SEG)
    table = table.transpose(1, 0, 2).reshape(channels, BAND, slot_count * SEG)
    south_side, north_side = table[:, :, :tile_cols], table[:, :, tile_cols : 2 * tile_cols]
    west_side = table[:, :, 2 * tile_cols : 2 * tile_cols + tile_rows]
    east_side = table[:, :, 2 * tile_cols + tile_rows :]
    state_hat = noisy_state.astype(jnp.float32) + spread * fresh_noise.astype(jnp.float32)
    net_in = jnp.concatenate(
        [scale_in * state_hat, conditioning.astype(jnp.float32)], axis=0
    ).astype(jnp.bfloat16)
    pairs_out = residual_block(
        net_in,
        *halos(net_in),
        first_weights(first_kernel, first_bias, film_weight, film_bias),
        second_weights(second_kernel),
        skip_weights(skip_kernel, second_bias),
        out_weights(out_kernel),
    )
    projected = pairs_out.reshape(tile_rows // 2, 2, channels, tile_cols)
    projected = projected.transpose(2, 0, 1, 3).reshape(channels, tile_rows, tile_cols)
    denoised = scale_skip * state_hat + scale_out * projected
    global_rows = (tile_row * tile_rows + jnp.arange(tile_rows, dtype=jnp.int32)).astype(
        jnp.float32
    )
    global_cols = (tile_col * tile_cols + jnp.arange(tile_cols, dtype=jnp.int32)).astype(
        jnp.float32
    )
    south_weight = relax_weight(global_rows, BAND)
    north_weight = relax_weight(total_rows - 1.0 - global_rows, BAND)
    west_weight = relax_weight(global_cols, BAND)
    east_weight = relax_weight(total_cols - 1.0 - global_cols, BAND)
    depths = jnp.arange(BAND, dtype=jnp.float32)[:, None]

    def placed(weight, distance):
        return jnp.where(distance[None, :] == depths, weight[None, :], 0.0).astype(jnp.bfloat16)

    by_row = jnp.concatenate(
        [
            placed(south_weight, global_rows),
            placed(north_weight, total_rows - 1.0 - global_rows),
        ],
        axis=0,
    )
    by_col = jnp.concatenate(
        [
            placed(west_weight, global_cols),
            placed(east_weight, total_cols - 1.0 - global_cols),
        ],
        axis=0,
    )
    every = (channels, 2 * BAND)
    along_rows = jnp.concatenate(
        [jnp.broadcast_to(by_row, every + by_row.shape[1:]), west_side, east_side], axis=1
    )
    along_cols = jnp.concatenate(
        [south_side, north_side, jnp.broadcast_to(by_col, every + by_col.shape[1:])], axis=1
    )
    targets = jnp.einsum("ckh,ckw->chw", along_rows, along_cols, preferred_element_type=jnp.float32)
    numerator = denoised + targets
    denominator = (
        1.0 + south_weight[:, None] + north_weight[:, None] + (west_weight + east_weight)[None, :]
    )
    relaxed = numerator / denominator[None]
    return (state_hat + stride * (state_hat - relaxed)).astype(jnp.bfloat16)


def solution(mesh):
    return jax.shard_map(
        on_device,
        mesh=mesh,
        in_specs=(
            P(None, "gy", "gx"),
            P(None, "gy", "gx"),
            P(None, "gy", "gx"),
            P(),
            P(),
            P(),
            P(),
            P(),
            P(),
            P(),
            P(),
            P("gx", None),
            P(),
            P(),
        ),
        out_specs=P(None, "gy", "gx"),
        check_vma=False,
    )
```
